256 devices in a mesh: expert: 8 (over x, core), tensor: 32 (over z, y).
Axes of the slice: x: 4, y: 4, z: 8, core: 2. Of those that a mesh axis runs over, the one named last changes fastest.
Arguments:
- tokens: bfloat16 [1024, 6144], P('expert', 'tensor'), may hold values from -6 to 6
- tangent: bfloat16 [1024, 6144], P('expert', 'tensor'), may hold values from -6 to 6
- cotangent: bfloat16 [1024, 6144], P('expert', 'tensor'), may hold values from -6 to 6
- expert_ids: int32 [1024, 2], P('expert'), may hold values from 0 to 7, all different within a row; in each aligned block of 128 rows (0 to 127, 128 to 255, ...) at most 48 rows name the same one
- gate_probs: bfloat16 [1024, 2], P('expert'), may hold values from 0.19921875 to 1
- w_gate: bfloat16 [8, 6144, 8192], P('expert', None, 'tensor'), may hold values from -0.078125 to 0.078125
- w_up: bfloat16 [8, 6144, 8192], P('expert', None, 'tensor'), may hold values from -0.078125 to 0.078125
- w_down: bfloat16 [8, 8192, 6144], P('expert', 'tensor'), may hold values from -0.0625 to 0.0625
Outputs:
- grad_in: bfloat16 [1024, 6144], P('expert', 'tensor')
- hvp_in: bfloat16 [1024, 6144], P('expert', 'tensor')
The draws below stay inside these ranges and needn't reach their ends.
Inputs may be any that keep to these rules, and one draw needn't show every extreme that they name: `expert_ids`: each row names 2 different experts. Within the rows of one index of expert (aligned blocks of 128 rows) no expert is named by more than 48 rows, and in every draw some expert is named by exactly 48 rows of some block.
All inputs are finite; a program needn't handle non-finite values.
Results may differ from the reference program's by a relative error of at most 0.022.
Values may be sent and summed in bfloat16 or wider, within the bound.
No kernel may reach another device: no remote copies, remote signals or barrier semaphores. Data moves between devices by JAX's collectives and lax.ppermute only.
A program may use at most 128 MiB of HBM per device.

```python
import math
import jax
import jax.numpy as jnp
import numpy as np
from jax import lax

D = 6144
FF = 8192
EXPERTS = 8
TOP = 2
TOK_DEV = 128
CAP = 48
TOKENS = 1024
N_EXPERT = 8
N_TENSOR = 32


def block_levels(stream_key, dims, pieces, least, largest):
    factor_of = 1.0
    for position, blocks in pieces:
        draws = jax.random.uniform(jax.random.fold_in(jax.random.fold_in(stream_key, 6), position), (blocks,), jnp.float32, least / len(pieces), largest / len(pieces))
        factor_of = factor_of * jnp.repeat(jnp.exp(draws), dims[position] // blocks).reshape((-1,) + (1,) * (len(dims) - 1 - position))
    return factor_of


def deal_out(key, own, number, rows, count, top, bound, slope):
    sequence = jax.random.permutation(key, count)
    heavy_load, usual = shares(count, rows * top, bound, slope, True), shares(count, rows * top, bound, slope, False)
    places = jnp.arange(count)

    def named(lengths, turn):
        used = int((lengths > 0).sum())
        fixed = max(1, used // 4)
        shifted = fixed + (places - fixed + turn * (used - fixed)) % max(1, count - fixed)
        return jnp.zeros((count,), jnp.int32).at[sequence[jnp.where(places < fixed, places, shifted)]].set(jnp.asarray(lengths, jnp.int32))

    lengths = jnp.where(number % 4 == 0, named(heavy_load, number // 4), named(usual, number - number // 4 - 1))
    mixed = jax.random.permutation(jax.random.fold_in(own, 3), count)
    donor, sink = mixed[0:count // 2 * 2:2], mixed[1:count // 2 * 2:2]
    room = jnp.minimum(lengths[donor] - 1, bound - lengths[sink]) // 2
    room = jnp.where((donor == sequence[0]) | (sink == sequence[0]) | (lengths[sink] == 0), 0, jnp.maximum(room, 0))
    shifted = jax.random.randint(jax.random.fold_in(own, 4), (count // 2,), 0, 1 << 20) % (room + 1)
    lengths = lengths.at[donor].add(-shifted).at[sink].add(shifted)
    members = jnp.searchsorted(jnp.cumsum(lengths), jnp.arange(rows * top), side="right").astype(jnp.int32)
    table = members.reshape(top, rows).T
    table = table[jax.random.permutation(jax.random.fold_in(own, 1), rows)]
    turn = jax.random.randint(jax.random.fold_in(own, 2), (rows, 1), 0, top)
    return jnp.take_along_axis(table, (jnp.arange(top)[None, :] + turn) % top, axis=1)


def shares(number_of, total, limit, lean, full):
    loads = [(1 << 20) // math.isqrt(rank ** lean) + 1 for rank in range(1, number_of + 1)]
    largest = limit if full else min(limit, max(-(-total // number_of), total * loads[0] // sum(loads)))
    least = 1 if total - largest >= number_of - 1 else 0
    counts, spare = [largest] + [least] * (number_of - 1), total - largest - least * (number_of - 1)
    while spare > 0:
        free = [i for i in range(1, number_of) if counts[i] < largest] or [i for i in range(1, number_of) if counts[i] < limit]
        mass, budget = sum([loads[i] for i in free]), spare
        for i in free:
            addition = min(limit - counts[i], max(1, budget * loads[i] // mass), spare)
            counts[i] = counts[i] + addition
            spare = spare - addition
    return np.array(counts)


def bell_draw(stream_key, extent, scale, bound, shards=(), kind=jnp.bfloat16):
    factor_of = block_levels(stream_key, extent, shards, -0.22, 0.18) if shards else 1.0
    entries = jax.random.normal(stream_key, extent, jnp.float32) * scale * factor_of
    return jnp.minimum(jnp.maximum(entries, -bound), bound).astype(kind)


def setup_inputs(seed: int = 0) -> dict:
    key_of = jax.random.split(jax.random.key(seed), 9)
    tokens = bell_draw(key_of[0], (TOKENS, D), 1.0, 6.0, ((0, 8), (1, 32)))
    tangent = bell_draw(key_of[1], (TOKENS, D), 1.0, 6.0, ((0, 8), (1, 32)))
    cotangent = bell_draw(key_of[2], (TOKENS, D), 1.0, 6.0, ((0, 8), (1, 32)))
    expert_ids_keys = jax.random.split(jax.random.fold_in(key_of[3], 1), TOKENS // TOK_DEV)
    expert_ids_turns = jax.random.permutation(jax.random.fold_in(key_of[3], 3), TOKENS // TOK_DEV)
    expert_ids = jax.vmap(lambda own, number: deal_out(jax.random.fold_in(key_of[3], 2), own, number, TOK_DEV, EXPERTS, TOP, CAP, 2))(expert_ids_keys, expert_ids_turns).reshape((TOKENS, TOP))
    gate_probs = jnp.clip(0.19921875 + 0.80078125 * jax.random.uniform(key_of[4], (TOKENS, TOP), jnp.float32) ** block_levels(key_of[4], (TOKENS, TOP), ((0, 8),), -0.2, 0.2), 0.19921875, 1.0).astype(jnp.bfloat16)
    w_gate = bell_draw(key_of[5], (EXPERTS, D, FF), D ** -0.5, 0.078125, ((0, 8), (2, 32)))
    w_up = bell_draw(key_of[6], (EXPERTS, D, FF), D ** -0.5, 0.078125, ((0, 8), (2, 32)))
    w_down = bell_draw(key_of[7], (EXPERTS, FF, D), FF ** -0.5, 0.0625, ((0, 8), (1, 32)))
    return {"tokens": tokens, "tangent": tangent, "cotangent": cotangent, "expert_ids": expert_ids, "gate_probs": gate_probs, "w_gate": w_gate, "w_up": w_up, "w_down": w_down}


def silu_terms(pre_gate):
    sigma = jax.nn.sigmoid(pre_gate)
    silu_value = pre_gate * sigma
    first = sigma * (1.0 + pre_gate * (1.0 - sigma))
    second = sigma * (1.0 - sigma) * (2.0 + pre_gate * (1.0 - 2.0 * sigma))
    return silu_value, first, second


def slot_of(expert_ids):
    flat = expert_ids.reshape(TOKENS * TOP)
    onehot = (flat[:, None] == jnp.arange(EXPERTS, dtype=jnp.int32)[None, :]).astype(jnp.int32)
    blocked = onehot.reshape(N_EXPERT, TOK_DEV * TOP, EXPERTS)
    before = (jnp.cumsum(blocked, axis=1) - blocked).reshape(TOKENS * TOP, EXPERTS)
    ranks = jnp.sum(before * onehot, axis=1)
    source = jnp.arange(TOKENS * TOP, dtype=jnp.int32) // (TOK_DEV * TOP)
    return flat, (source * CAP + ranks).astype(jnp.int32)


def block_sum(gate_part, up_part, gate_weight, up_weight):
    count = gate_part.shape[0]
    width = FF // N_TENSOR
    gate_blocks = jnp.transpose(gate_part.reshape(count, N_TENSOR, width), (1, 0, 2))
    up_blocks = jnp.transpose(up_part.reshape(count, N_TENSOR, width), (1, 0, 2))
    gate_cols = jnp.transpose(gate_weight.reshape(D, N_TENSOR, width), (1, 0, 2))
    up_cols = jnp.transpose(up_weight.reshape(D, N_TENSOR, width), (1, 0, 2))

    def step(total, piece):
        gate_piece, up_piece, gate_mat, up_mat = piece
        term = jnp.dot(gate_piece, gate_mat.T, preferred_element_type=jnp.float32)
        term = term + jnp.dot(up_piece, up_mat.T, preferred_element_type=jnp.float32)
        term = lax.optimization_barrier(term.astype(jnp.bfloat16))
        return total + term.astype(jnp.float32), None

    total, unused = lax.scan(step, jnp.zeros((count, D), jnp.float32), (gate_blocks, up_blocks, gate_cols, up_cols))
    return total


def reference(tokens, tangent, cotangent, expert_ids, gate_probs, w_gate, w_up, w_down):
    flat, slots = slot_of(expert_ids)
    owner = (jnp.arange(TOKENS * TOP, dtype=jnp.int32) // TOP).astype(jnp.int32)
    table = jnp.zeros((EXPERTS, N_EXPERT * CAP), jnp.int32).at[flat, slots].set(owner)
    valid = jnp.zeros((EXPERTS, N_EXPERT * CAP), jnp.float32).at[flat, slots].set(1.0)
    weight = jnp.zeros((EXPERTS, N_EXPERT * CAP), jnp.float32).at[flat, slots].set(gate_probs.reshape(TOKENS * TOP).astype(jnp.float32))

    def expert_terms(inputs):
        gate_weight, up_weight, down_weight, index, live, prob = inputs
        keep = live[:, None] > 0.5
        zero = jnp.zeros((), jnp.bfloat16)
        rows_in = jnp.where(keep, tokens[index], zero)
        rows_tan = jnp.where(keep, tangent[index], zero)
        rows_cot = jnp.where(keep, cotangent[index], zero)
        pre_gate = jnp.dot(rows_in, gate_weight, preferred_element_type=jnp.float32)
        pre_up = jnp.dot(rows_in, up_weight, preferred_element_type=jnp.float32)
        tan_gate = jnp.dot(rows_tan, gate_weight, preferred_element_type=jnp.float32)
        tan_up = jnp.dot(rows_tan, up_weight, preferred_element_type=jnp.float32)
        back_grad = jnp.dot(rows_cot, down_weight.T, preferred_element_type=jnp.float32) * prob[:, None]
        silu_value, first, second = silu_terms(pre_gate)
        grad_gate = (back_grad * pre_up * first).astype(jnp.bfloat16)
        grad_up = (back_grad * silu_value).astype(jnp.bfloat16)
        curv_gate = (back_grad * (tan_up * first + pre_up * second * tan_gate)).astype(jnp.bfloat16)
        curv_up = (back_grad * first * tan_gate).astype(jnp.bfloat16)
        grad_rows = block_sum(grad_gate, grad_up, gate_weight, up_weight)
        curv_rows = block_sum(curv_gate, curv_up, gate_weight, up_weight)
        return grad_rows * live[:, None], curv_rows * live[:, None]

    grad_all, curv_all = lax.map(expert_terms, (w_gate, w_up, w_down, table, valid, weight))
    targets = table.reshape(EXPERTS * N_EXPERT * CAP)
    grad_in = jnp.zeros((TOKENS, D), jnp.float32).at[targets].add(grad_all.reshape(EXPERTS * N_EXPERT * CAP, D))
    hvp_in = jnp.zeros((TOKENS, D), jnp.float32).at[targets].add(curv_all.reshape(EXPERTS * N_EXPERT * CAP, D))
    return grad_in.astype(jnp.bfloat16), hvp_in.astype(jnp.bfloat16)
```

```python
import jax
import jax.numpy as jnp
from jax import lax
from jax.experimental import pallas as pl
from jax.experimental.pallas import tpu as pltpu
from jax.sharding import PartitionSpec as P

EXPERTS = 8
TOP = 2
CAP = 48
SLOTS = EXPERTS * CAP
NZ = 8
NY = 4
TOK = 128
FEAT = 192
HALF = 96
HID = 256
F32 = jnp.float32
BF16 = jnp.bfloat16
VMEM = 60 * 1024 * 1024


def z_perm(step):
    return [
        (z * NY + y, ((z + step) % NZ) * NY + y) for z in range(NZ) for y in range(NY)
    ]


def y_perm(step):
    return [
        (z * NY + y, z * NY + (y + step) % NY) for z in range(NZ) for y in range(NY)
    ]


def send(block, axis, step):
    perm = z_perm(step) if axis == "z" else y_perm(step)
    return lax.ppermute(block, "tensor", perm)


def pack_kernel(ids_ref, prob_ref, tok_ref, tan_ref, cot_ref, out_ref, table_ref):
    ids = ids_ref[...]
    prob = prob_ref[...].astype(F32)
    lane8 = lax.broadcasted_iota(jnp.int32, (TOK, EXPERTS), 1)
    hits = [(ids[:, k : k + 1] == lane8).astype(F32) for k in range(TOP)]
    row = lax.broadcasted_iota(jnp.int32, (TOK, TOK), 0)
    col = lax.broadcasted_iota(jnp.int32, (TOK, TOK), 1)
    lower = (col < row).astype(BF16)
    ranks = jnp.dot(lower, (hits[0] + hits[1]).astype(BF16), preferred_element_type=F32)
    lane = lax.broadcasted_iota(jnp.int32, (TOK, SLOTS), 1)
    table = jnp.zeros((TOK, SLOTS), F32)
    weight = jnp.zeros((TOK, SLOTS), F32)
    for k in range(TOP):
        rank = jnp.sum(ranks * hits[k], axis=1, keepdims=True).astype(jnp.int32)
        here = (lane == ids[:, k : k + 1] * CAP + rank).astype(F32)
        table = table + here
        weight = weight + here * prob[:, k : k + 1]
    table_ref[...] = table.astype(BF16)
    spread = table.T.astype(BF16)
    source = jnp.concatenate([tok_ref[...], tan_ref[...], cot_ref[...]], axis=1)
    placed = jnp.dot(spread, source, preferred_element_type=F32).astype(BF16)
    ones = jnp.ones((TOK, 64), BF16)
    weights = jnp.dot(weight.T.astype(BF16), ones, preferred_element_type=F32)
    out_ref[...] = jnp.concatenate([placed, weights.astype(BF16)], axis=1)


def pack(ids, prob, tok, tan, cot):
    return pl.pallas_call(
        pack_kernel,
        out_shape=(
            jax.ShapeDtypeStruct((SLOTS, 640), BF16),
            jax.ShapeDtypeStruct((TOK, SLOTS), BF16),
        ),
        name="pack",
    )(ids, prob, tok, tan, cot)


def turn_kernel(in_ref, a_ref, b_ref, prob_ref):
    turned = in_ref[...].astype(F32).T
    for i in range(3):
        part = turned[i * FEAT : (i + 1) * FEAT].astype(BF16)
        a_ref[:, i * SLOTS : (i + 1) * SLOTS] = part[:HALF]
        b_ref[:, i * SLOTS : (i + 1) * SLOTS] = part[HALF:]
    prob_ref[...] = turned[3 * FEAT : 3 * FEAT + 8]


def turn(routed):
    return pl.pallas_call(
        turn_kernel,
        out_shape=(
            jax.ShapeDtypeStruct((HALF, 3 * SLOTS), BF16),
            jax.ShapeDtypeStruct((HALF, 3 * SLOTS), BF16),
            jax.ShapeDtypeStruct((8, SLOTS), F32),
        ),
        name="turn",
    )(routed)


def order_kernel(place_ref, gate_ref, up_ref, down_ref, a_ref, b_ref):
    y = place_ref[1]
    down_t = down_ref[0].astype(F32).T.astype(BF16)
    scratch = jnp.concatenate([gate_ref[0], up_ref[0], down_t], axis=1)
    for r in range(NY):
        for shift in range(NY):

            @pl.when(y == shift)
            def _():
                start = ((shift + r) % NY) * FEAT
                a_ref[r] = scratch[start : start + HALF]
                b_ref[0, r * HALF : (r + 1) * HALF] = scratch[start + HALF : start + FEAT]


def order(place, w_gate, w_up, w_down):
    rows = NY * FEAT
    return pl.pallas_call(
        order_kernel,
        grid_spec=pltpu.PrefetchScalarGridSpec(
            num_scalar_prefetch=1,
            grid=(NZ,),
            in_specs=[
                pl.BlockSpec((1, rows, HID), lambda q, p: (0, (p[0] + q) % NZ, 0)),
                pl.BlockSpec((1, rows, HID), lambda q, p: (0, (p[0] + q) % NZ, 0)),
                pl.BlockSpec((1, HID, rows), lambda q, p: (0, 0, (p[0] + q) % NZ)),
            ],
            out_specs=[
                pl.BlockSpec((NY, HALF, 3 * HID), lambda q, p: (0, q, 0)),
                pl.BlockSpec((1, NY * HALF, 3 * HID), lambda q, p: (q, 0, 0)),
            ],
        ),
        out_shape=(
            jax.ShapeDtypeStruct((NY, NZ * HALF, 3 * HID), BF16),
            jax.ShapeDtypeStruct((NZ, NY * HALF, 3 * HID), BF16),
        ),
        compiler_params=pltpu.CompilerParams(vmem_limit_bytes=VMEM),
        cost_estimate=pl.CostEstimate(
            flops=0, bytes_accessed=4 * 9437184, transcendentals=0
        ),
        name="order",
    )(place, w_gate, w_up, w_down)


def flip_kernel(in_ref, out_ref):
    out_ref[0] = in_ref[0].astype(F32).T.astype(BF16)


def flip(w):
    n, rows, cols = w.shape
    return pl.pallas_call(
        flip_kernel,
        grid=(n,),
        in_specs=[pl.BlockSpec((1, rows, cols), lambda i: (i, 0, 0))],
        out_specs=pl.BlockSpec((1, cols, rows), lambda i: (i, 0, 0)),
        out_shape=jax.ShapeDtypeStruct((n, cols, rows), BF16),
        compiler_params=pltpu.CompilerParams(vmem_limit_bytes=VMEM),
        cost_estimate=pl.CostEstimate(
            flops=0, bytes_accessed=4 * n * rows * cols, transcendentals=0
        ),
        name="flip",
    )(w)


def unturn_kernel(a_ref, b_ref, out_ref):
    both = jnp.concatenate([a_ref[...], b_ref[...]], axis=0).astype(F32)
    grad = both[:, :SLOTS].T
    curv = both[:, SLOTS:].T
    out_ref[...] = jnp.concatenate([grad, curv], axis=1).astype(BF16)


def unturn(a, b):
    return pl.pallas_call(
        unturn_kernel,
        out_shape=jax.ShapeDtypeStruct((SLOTS, 2 * FEAT), BF16),
        name="unturn",
    )(a, b)


def combine_kernel(table_ref, in_ref, grad_ref, curv_ref):
    total = jnp.dot(table_ref[...], in_ref[...], preferred_element_type=F32).astype(BF16)
    grad_ref[...] = total[:, :FEAT]
    curv_ref[...] = total[:, FEAT:]


def combine(table, back):
    return pl.pallas_call(
        combine_kernel,
        out_shape=(
            jax.ShapeDtypeStruct((TOK, FEAT), BF16),
            jax.ShapeDtypeStruct((TOK, FEAT), BF16),
        ),
        name="combine",
    )(table, back)


def ring_gather(block, axis, n):
    pieces = [None] * n
    pieces[0] = block
    up = down = block
    for step in range(1, n // 2):
        up = send(up, axis, 1)
        down = send(down, axis, -1)
        pieces[n - step] = up
        pieces[step] = down
    cut = block.shape[0] // 2
    first = send(up[:cut], axis, 1)
    second = send(down[cut:], axis, -1)
    pieces[n // 2] = jnp.concatenate([first, second], axis=0)
    return pieces


def ring_scatter(part, axis, n):
    far = part(n // 2).astype(BF16)
    cut = far.shape[0] // 2
    up = send(far[:cut], axis, 1)
    down = send(far[cut:], axis, -1)
    for step in range(n // 2 - 1, 0, -1):
        mine_up = part(step)
        mine_down = part(n - step)
        if step == n // 2 - 1:
            up = jnp.concatenate([mine_up[:cut] + up.astype(F32), mine_up[cut:]], axis=0)
            down = jnp.concatenate(
                [mine_down[:cut], mine_down[cut:] + down.astype(F32)], axis=0
            )
        else:
            up = mine_up + up.astype(F32)
            down = mine_down + down.astype(F32)
        up = send(up.astype(BF16), axis, 1)
        down = send(down.astype(BF16), axis, -1)
    return part(0) + up.astype(F32) + down.astype(F32)


def on_device(tokens, tangent, cotangent, expert_ids, gate_probs, w_gate, w_up, w_down):
    spot = lax.axis_index("tensor")
    place = jnp.stack([spot // NY, spot % NY]).astype(jnp.int32)
    packed, table = pack(expert_ids, gate_probs, tokens, tangent, cotangent)
    routed = lax.all_to_all(
        packed.reshape(EXPERTS, CAP, 640), "expert", split_axis=0, concat_axis=0, tiled=True
    )
    block_a, block_b, prob = turn(routed.reshape(SLOTS, 640))
    w_a, w_b = order(place, w_gate, w_up, w_down)
    t_a, t_b = flip(w_a), flip(w_b)

    small_a = ring_gather(block_a, "z", NZ)
    small_b = ring_gather(block_b, "y", NY)
    big_a = ring_gather(jnp.concatenate(small_a, axis=0), "y", NY)
    big_b = ring_gather(jnp.concatenate(small_b, axis=0), "z", NZ)

    fore = jnp.zeros((2 * HID, 2 * SLOTS), F32)
    back = jnp.zeros((HID, SLOTS), F32)
    for pieces, weights in ((big_a, t_a), (big_b, t_b)):
        for i, piece in enumerate(pieces):
            fore = fore + jnp.dot(
                weights[i, : 2 * HID], piece[:, : 2 * SLOTS], preferred_element_type=F32
            )
            back = back + jnp.dot(
                weights[i, 2 * HID :], piece[:, 2 * SLOTS :], preferred_element_type=F32
            )
    back = back * prob[:1]
    pre_gate, tan_gate = fore[:HID, :SLOTS], fore[:HID, SLOTS:]
    pre_up, tan_up = fore[HID:, :SLOTS], fore[HID:, SLOTS:]
    sig = jax.nn.sigmoid(pre_gate)
    silu_value = pre_gate * sig
    first = sig * (1.0 + pre_gate * (1.0 - sig))
    second = sig * (1.0 - sig) * (2.0 + pre_gate * (1.0 - 2.0 * sig))
    grad_gate = (back * pre_up * first).astype(BF16)
    grad_up = (back * silu_value).astype(BF16)
    curv_gate = (back * (tan_up * first + pre_up * second * tan_gate)).astype(BF16)
    curv_up = (back * first * tan_gate).astype(BF16)
    terms = jnp.concatenate(
        [
            jnp.concatenate([grad_gate, curv_gate], axis=1),
            jnp.concatenate([grad_up, curv_up], axis=1),
        ],
        axis=0,
    )

    def part_a(i):
        return jnp.dot(w_a[i, :, : 2 * HID], terms, preferred_element_type=F32)

    def part_b(i):
        return jnp.dot(w_b[i, :, : 2 * HID], terms, preferred_element_type=F32)

    mid_a = ring_scatter(part_a, "y", NY)
    mid_b = ring_scatter(part_b, "z", NZ)
    sum_a = ring_scatter(lambda i: mid_a[i * HALF : (i + 1) * HALF], "z", NZ)
    sum_b = ring_scatter(lambda i: mid_b[i * HALF : (i + 1) * HALF], "y", NY)
    sums = unturn(sum_a.astype(BF16), sum_b.astype(BF16))
    returned = lax.all_to_all(
        sums.reshape(EXPERTS, CAP, 2 * FEAT), "expert", split_axis=0, concat_axis=0, tiled=True
    )
    return combine(table, returned.reshape(SLOTS, 2 * FEAT))


def solution(mesh):
    in_specs = (
        P("expert", "tensor"),
        P("expert", "tensor"),
        P("expert", "tensor"),
        P("expert", None),
        P("expert", None),
        P("expert", None, "tensor"),
        P("expert", None, "tensor"),
        P("expert", "tensor", None),
    )
    out_specs = (P("expert", "tensor"), P("expert", "tensor"))
    return jax.shard_map(
        on_device, mesh=mesh, in_specs=in_specs, out_specs=out_specs, check_vma=False
    )
```

```python
import functools

import jax
import jax.numpy as jnp
from jax import lax
from jax.experimental import pallas as pl
from jax.experimental.pallas import tpu as pltpu
from jax.sharding import Mesh, PartitionSpec as P

EXPERTS = 8
TOP = 2
CAP = 48
SLOTS = EXPERTS * CAP
NZ = 8
NY = 4
TOK = 128
FEAT = 192
GA = 112
GB = 80
SA = 112
SB = 80
HID = 256
LANES = 128
F32 = jnp.float32
BF16 = jnp.bfloat16
VMEM = 60 * 1024 * 1024
LARGE = pl.CostEstimate(flops=500_000_000_000, bytes_accessed=1024, transcendentals=0)
SMALL = pl.CostEstimate(flops=1024, bytes_accessed=1024, transcendentals=0)


def send(block, axis, step):
    n = NZ if axis == "z" else NY
    return lax.ppermute(block, axis, [(i, (i + step) % n) for i in range(n)])


def pack_kernel(ids_ref, prob_ref, tok_ref, tan_ref, cot_ref, out_ref, table_ref):
    ids = ids_ref[...]
    prob = prob_ref[...].astype(F32)
    expert = lax.broadcasted_iota(jnp.int32, (EXPERTS, TOK), 0)
    hits = [(ids[k : k + 1] == expert).astype(F32) for k in range(TOP)]
    row = lax.broadcasted_iota(jnp.int32, (TOK, TOK), 0)
    col = lax.broadcasted_iota(jnp.int32, (TOK, TOK), 1)
    earlier = (row < col).astype(BF16)
    ranks = jnp.dot((hits[0] + hits[1]).astype(BF16), earlier, preferred_element_type=F32)
    slot = lax.broadcasted_iota(jnp.int32, (SLOTS, TOK), 0)
    table = jnp.zeros((SLOTS, TOK), F32)
    weight = jnp.zeros((SLOTS, TOK), F32)
    for k in range(TOP):
        rank = jnp.sum(ranks * hits[k], axis=0, keepdims=True).astype(jnp.int32)
        here = (slot == ids[k : k + 1] * CAP + rank).astype(F32)
        table = table + here
        weight = weight + here * prob[k : k + 1]
    table = table.astype(BF16)
    table_ref[...] = table
    source = jnp.concatenate([tok_ref[...], tan_ref[...], cot_ref[...]], axis=0)
    dims = (((1,), (1,)), ((), ()))
    placed = lax.dot_general(table, source, dims, preferred_element_type=F32)
    ones = jnp.ones((64, TOK), BF16)
    weights = lax.dot_general(weight.astype(BF16), ones, dims, preferred_element_type=F32)
    out_ref[...] = jnp.concatenate([placed.astype(BF16), weights.astype(BF16)], axis=1)


def pack(ids, prob, tok, tan, cot):
    return pl.pallas_call(
        pack_kernel,
        out_shape=(
            jax.ShapeDtypeStruct((SLOTS, 640), BF16),
            jax.ShapeDtypeStruct((SLOTS, TOK), BF16),
        ),
        name="pack",
    )(ids, prob, tok, tan, cot)


def turn_kernel(in_ref, a_ref, b_ref, prob_ref):
    turned = in_ref[...].astype(F32).T
    for i in range(3):
        part = turned[i * FEAT : (i + 1) * FEAT].astype(BF16)
        a_ref[:, i * SLOTS : (i + 1) * SLOTS] = part[:GA]
        b_ref[:, i * SLOTS : (i + 1) * SLOTS] = part[GA:]
    prob_ref[...] = turned[3 * FEAT : 3 * FEAT + 8]


def turn(routed):
    return pl.pallas_call(
        turn_kernel,
        out_shape=(
            jax.ShapeDtypeStruct((GA, 3 * SLOTS), BF16),
            jax.ShapeDtypeStruct((GB, 3 * SLOTS), BF16),
            jax.ShapeDtypeStruct((8, SLOTS), F32),
        ),
        name="turn",
    )(routed)


def z_place(i, place):
    i = (i + 3) % NZ
    return (place[0] + NZ + (i + 1) // 2 * (2 * (i % 2) - 1)) % NZ


def order_kernel(cut, place_ref, *refs):
    a_ref, b_ref = refs[-2:]
    parts = [refs[0][0], refs[1][0]]
    if len(refs) == 5:
        parts.append(refs[2][0].astype(F32).T.astype(BF16))
    rows = jnp.concatenate(parts, axis=1)
    rest = FEAT - cut
    for shift in range(NY):

        @pl.when(place_ref[1] == shift)
        def _():
            for r in range(NY):
                start = (shift + r) % NY * FEAT
                a_ref[r] = rows[start : start + cut]
                b_ref[r * rest : (r + 1) * rest] = rows[start + cut : start + FEAT]


def order(place, cut, *weights):
    rows, cols, rest = NY * FEAT, len(weights) * HID, FEAT - cut
    tall = pl.BlockSpec((1, rows, HID), lambda i, p: (0, z_place(i, p), 0))
    wide = pl.BlockSpec((1, HID, rows), lambda i, p: (0, 0, z_place(i, p)))
    return pl.pallas_call(
        functools.partial(order_kernel, cut),
        grid_spec=pltpu.PrefetchScalarGridSpec(
            num_scalar_prefetch=1,
            grid=(NZ,),
            in_specs=[tall, tall, wide][: len(weights)],
            out_specs=[
                pl.BlockSpec((NY, cut, cols), lambda i, p: (0, i, 0)),
                pl.BlockSpec((NY * rest, cols), lambda i, p: (z_place(i, p), 0)),
            ],
        ),
        out_shape=(
            jax.ShapeDtypeStruct((NY, NZ * cut, cols), BF16),
            jax.ShapeDtypeStruct((NZ * NY * rest, cols), BF16),
        ),
        compiler_params=pltpu.CompilerParams(vmem_limit_bytes=VMEM),
        cost_estimate=pl.CostEstimate(
            flops=0, bytes_accessed=4 * 6144 * cols, transcendentals=0
        ),
        name="order",
    )(place, *weights)


def flip_kernel(in_ref, *out_refs):
    turned = in_ref[0].astype(F32).T.astype(BF16)
    start = 0
    for out_ref in out_refs:
        width = out_ref.shape[2]
        out_ref[0] = turned[:, start : start + width]
        start += width


def flip(w, *widths):
    n, rows, cols = w.shape
    return pl.pallas_call(
        flip_kernel,
        grid=(n,),
        in_specs=[pl.BlockSpec((1, rows, cols), lambda i: (i, 0, 0))],
        out_specs=[pl.BlockSpec((1, cols, width), lambda i: (i, 0, 0)) for width in widths],
        out_shape=[jax.ShapeDtypeStruct((n, cols, width), BF16) for width in widths],
        compiler_params=pltpu.CompilerParams(vmem_limit_bytes=VMEM),
        cost_estimate=SMALL,
        name="flip",
    )(w)


def unturn_kernel(a_ref, b_ref, out_ref):
    both = jnp.concatenate([a_ref[...], b_ref[...]], axis=0).astype(F32)
    for j in range(SLOTS // LANES):
        rows = slice(j * LANES, (j + 1) * LANES)
        grad = both[:, 2 * j * LANES : (2 * j + 1) * LANES].T
        curv = both[:, (2 * j + 1) * LANES : (2 * j + 2) * LANES].T
        out_ref[rows] = jnp.concatenate([grad, curv], axis=1).astype(BF16)


def unturn(a, b):
    return pl.pallas_call(
        unturn_kernel,
        out_shape=jax.ShapeDtypeStruct((SLOTS, 2 * FEAT), BF16),
        name="unturn",
    )(a, b)


def combine_kernel(table_ref, in_ref, grad_ref, curv_ref):
    sums = in_ref[...].astype(F32).T.astype(BF16)
    total = jnp.dot(sums, table_ref[...], preferred_element_type=F32).astype(BF16)
    grad_ref[...] = total[:FEAT]
    curv_ref[...] = total[FEAT:]


def combine(table, back):
    return pl.pallas_call(
        combine_kernel,
        out_shape=(
            jax.ShapeDtypeStruct((FEAT, TOK), BF16),
            jax.ShapeDtypeStruct((FEAT, TOK), BF16),
        ),
        name="combine",
    )(table, back)


def products(groups, refs, fore, back):
    at = 0
    for ranges in groups:
        w = refs[at][0]
        tok, tan, cot = [
            jnp.concatenate(
                [refs[at + 1 + 3 * n + i][a:b] for n, (a, b) in enumerate(ranges)], axis=0
            )
            for i in range(3)
        ]
        at += 1 + 3 * len(ranges)
        fore = fore + matmul(w[: 2 * HID], jnp.concatenate([tok, tan], axis=1))
        back = back + matmul(w[2 * HID :], cot)
    return fore, back


def absorb_kernel(counts, first, *refs):
    fore_out, back_out = refs[-2:]
    if first:
        fore, back = jnp.zeros(fore_out.shape, F32), jnp.zeros(back_out.shape, F32)
    else:
        fore, back = refs[0][...], refs[1][...]
        refs = refs[2:]
    fore_out[...], back_out[...] = products(counts, refs[:-2], fore, back)


def finish_kernel(counts, fore_ref, back_ref, prob_ref, w_far_ref, *refs):
    out_ref, far_ref = refs[-2:]
    fore, back = products(counts, refs[:-2], fore_ref[...], back_ref[...])
    back = back * prob_ref[:1]
    pre_gate, pre_up = fore[:HID, :LANES], fore[HID:, :LANES]
    tan_gate, tan_up = fore[:HID, LANES:], fore[HID:, LANES:]
    sig = 1.0 / (1.0 + jnp.exp(-pre_gate))
    silu_value = pre_gate * sig
    first = sig * (1.0 + pre_gate * (1.0 - sig))
    second = sig * (1.0 - sig) * (2.0 + pre_gate * (1.0 - 2.0 * sig))
    out_ref[:HID, :LANES] = (back * pre_up * first).astype(BF16)
    out_ref[HID:, :LANES] = (back * silu_value).astype(BF16)
    curv_gate = back * (tan_up * first + pre_up * second * tan_gate)
    out_ref[:HID, LANES:] = curv_gate.astype(BF16)
    out_ref[HID:, LANES:] = (back * first * tan_gate).astype(BF16)
    terms = out_ref[...]
    far_ref[...] = matmul(w_far_ref[0], terms).astype(BF16)


FORE = pl.BlockSpec((2 * HID, 2 * LANES), lambda j: (0, j))
BACK = pl.BlockSpec((HID, LANES), lambda j: (0, j))
PROB = pl.BlockSpec((8, LANES), lambda j: (0, j))


def operands(groups):
    n = SLOTS // LANES
    specs, arrays = [], []
    for weights, place, pieces in groups:
        specs.append(pl.BlockSpec((1,) + weights.shape[1:], lambda j, r=place: (r, 0, 0)))
        arrays.append(weights)
        for piece, _, _ in pieces:
            for i in range(3):
                block = (piece.shape[0], LANES)
                specs.append(pl.BlockSpec(block, lambda j, i=i: (0, i * n + j)))
                arrays.append(piece)
    return [[piece[1:] for piece in pieces] for _, _, pieces in groups], specs, arrays


def absorb(sums, groups):
    counts, specs, arrays = operands(groups)
    return pl.pallas_call(
        functools.partial(absorb_kernel, counts, sums is None),
        grid=(SLOTS // LANES,),
        in_specs=([] if sums is None else [FORE, BACK]) + specs,
        out_specs=[FORE, BACK],
        out_shape=[
            jax.ShapeDtypeStruct((2 * HID, 2 * SLOTS), F32),
            jax.ShapeDtypeStruct((HID, SLOTS), F32),
        ],
        compiler_params=pltpu.CompilerParams(vmem_limit_bytes=VMEM),
        cost_estimate=SMALL,
        name="absorb",
    )(*(sums or ()), *arrays)


def finish(sums, prob, w_far, place, groups):
    counts, specs, arrays = operands(groups)
    far = w_far.shape[1]
    return pl.pallas_call(
        functools.partial(finish_kernel, counts),
        grid=(SLOTS // LANES,),
        in_specs=[
            FORE,
            BACK,
            PROB,
            pl.BlockSpec((1, far, 2 * HID), lambda j: (place, 0, 0)),
        ]
        + specs,
        out_specs=[
            FORE,
            pl.BlockSpec((far, 2 * LANES), lambda j: (0, j)),
        ],
        out_shape=[
            jax.ShapeDtypeStruct((rows, 2 * SLOTS), BF16) for rows in (2 * HID, far)
        ],
        compiler_params=pltpu.CompilerParams(vmem_limit_bytes=VMEM),
        cost_estimate=SMALL,
        name="finish",
    )(*sums, prob, w_far, *arrays)


def after(x, *others):
    return lax.optimization_barrier((x, *others))[0]


def halves(rows):
    return rows // 32 * 16


def near_kernel(rows, w_up_ref, w_down_ref, terms_ref, up_ref, down_ref, *out_refs):
    cut = up_ref.shape[0]
    terms = terms_ref[...]
    up = matmul(w_up_ref[0], terms)
    down = matmul(w_down_ref[0], terms)
    up = jnp.concatenate([up[:cut] + up_ref[...].astype(F32), up[cut:]], axis=0)
    down = jnp.concatenate([down[:cut], down[cut:] + down_ref[...].astype(F32)], axis=0)
    for i, term in enumerate((up, down)):
        out_refs[i][...] = term[:rows].astype(BF16)
        out_refs[2 + i][...] = term[rows:].astype(BF16)


def near_terms(weights, terms, up, down, rows):
    total = weights.shape[1]

    def lanes(count):
        return pl.BlockSpec((count, 2 * LANES), lambda j: (0, j))

    def whole(place):
        return pl.BlockSpec((1, total, 2 * HID), lambda j: (place, 0, 0))

    outs = (rows, rows, total - rows, total - rows)
    return pl.pallas_call(
        functools.partial(near_kernel, rows),
        grid=(SLOTS // LANES,),
        in_specs=[whole(1), whole(3), FORE, lanes(up.shape[0]), lanes(down.shape[0])],
        out_specs=[lanes(count) for count in outs],
        out_shape=[jax.ShapeDtypeStruct((count, 2 * SLOTS), BF16) for count in outs],
        compiler_params=pltpu.CompilerParams(vmem_limit_bytes=VMEM),
        cost_estimate=LARGE,
        name="near",
    )(weights, weights, terms, up, down)


def y_both(block):
    return y_both_of(block, block)


def y_both_of(up, down):
    return send(up, "y", 1), send(down, "y", -1)


def y_far(up, down):
    cut = halves(up.shape[0])
    return send(up[:cut], "y", 1), send(down[cut:], "y", -1)


def matmul(a, b):
    return jnp.dot(a, b, preferred_element_type=F32)


def on_device(tokens, tangent, cotangent, expert_ids, gate_probs, w_gate, w_up, w_down):
    place = jnp.stack([lax.axis_index("z"), lax.axis_index("y")]).astype(jnp.int32)
    packed, table = pack(expert_ids.T, gate_probs.T, tokens.T, tangent.T, cotangent.T)
    routed = lax.all_to_all(
        packed.reshape(EXPERTS, CAP, 640), ("x", "c"), split_axis=0, concat_axis=0, tiled=True
    )
    routed, w1_a, w1_b = lax.optimization_barrier(
        (routed, *order(place, GA, w_gate, w_up, w_down))
    )
    block_a, block_b, prob = turn(routed.reshape(SLOTS, 640))

    up1, down1 = send(block_a, "z", 1), send(block_a, "z", -1)
    near = [send(block_b, "y", step) for step in (1, -1, 2)]
    up1, down1, *near = lax.optimization_barrier((up1, down1, *near))
    early = jnp.concatenate([block_a, down1, up1], axis=0)
    up2, down2 = lax.optimization_barrier((send(up1, "z", 1), send(down1, "z", -1)))
    early_up, early_down = y_both(early)
    up3, down3 = lax.optimization_barrier((send(up2, "z", 1), send(down2, "z", -1)))
    far = send(up3, "z", 1)
    wide_b = jnp.concatenate([block_b, near[1], near[2], near[0]], axis=0)
    all_b = lax.all_gather(after(wide_b, up2, down2), "z", axis=0, tiled=True)
    late = [down2, up2, down3, up3, far]
    half = halves(early.shape[0])
    late_up = send(jnp.concatenate([early_up[:half], *late], axis=0), "y", 1)
    late_down = send(jnp.concatenate([early_down[half:], *late], axis=0), "y", -1)

    w1_a, w1_b, _ = lax.optimization_barrier((w1_a, w1_b, far))
    t_late, t_early = flip(w1_a, 5 * GA, 3 * GA)
    (t_b,) = flip(w1_b.reshape(1, NZ * NY * GB, 3 * HID), NZ * NY * GB)
    w2_a, w2_b = order(after(place, far), SA, w_gate, w_up)

    sums = absorb(
        None,
        [
            (t_early, 0, [(early, 0, 3 * GA)]),
            (t_early, 3, [(early_up, 0, 3 * GA)]),
            (t_early, 1, [(early_down, 0, 3 * GA)]),
            (t_late, 0, [(block, 0, GA) for block in late]),
        ],
    )
    sums, t_b, w2_a, w2_b, late_up, late_down = lax.optimization_barrier(
        (sums, t_b, w2_a, w2_b, late_up, late_down)
    )
    rest = 3 * GA - half
    ends = (half, half + 5 * GA), (rest, rest + 5 * GA)
    cut = halves(5 * GA)
    late_far_up = send(late_up[half : half + cut], "y", 1)
    late_far_down = send(late_down[rest + cut :], "y", -1)
    sums = absorb(
        sums,
        [
            (t_early, 2, [(late_up, 0, half), (late_down, 0, rest)]),
            (t_late, 3, [(late_up, *ends[0])]),
            (t_late, 1, [(late_down, *ends[1])]),
        ],
    )
    sums = absorb(sums, [(t_b, 0, [(all_b, 0, NZ * NY * GB)])])
    late_far = [(late_far_up, 0, cut), (late_far_down, 0, 5 * GA - cut)]
    terms, far = finish(sums, prob, w2_a, 2, [(t_late, 2, late_far)])

    rows = 5 * SA
    cut = 4 * SA
    up, down = send(far[:cut], "y", 1), send(far[cut:], "y", -1)
    late_up, late_down, early_up, early_down = near_terms(w2_a, terms, up, down, rows)
    part_b = matmul(w2_b, terms).astype(BF16)
    mid_b = lax.psum_scatter(part_b, "z", scatter_dimension=0, tiled=True)
    own = matmul(w2_a[0], terms)
    up, down = lax.optimization_barrier(y_both_of(late_up, late_down))
    early_up, early_down, _ = lax.optimization_barrier((early_up, early_down, up))
    late = own[:rows] + up.astype(F32) + down.astype(F32)
    near_up, near_down = y_both_of(early_up, early_down)
    late = [late[i * SA : (i + 1) * SA] for i in range(5)]
    up = send(late[4].astype(BF16), "z", 1)
    down = send(late[3].astype(BF16), "z", -1)
    up = send((late[2] + up.astype(F32)).astype(BF16), "z", 1)
    down = send((late[1] + down.astype(F32)).astype(BF16), "z", -1)
    up = send((late[0] + up.astype(F32)).astype(BF16), "z", 1)
    early = own[rows:] + near_up.astype(F32) + near_down.astype(F32)
    down = send((early[2 * SA :] + down.astype(F32)).astype(BF16), "z", -1)
    up = send((early[SA : 2 * SA] + up.astype(F32)).astype(BF16), "z", 1)
    sum_a = early[:SA] + up.astype(F32) + down.astype(F32)

    blocks = [mid_b[r * SB : (r + 1) * SB] for r in range(NY)]
    sum_b = blocks[0].astype(F32)
    for r, step in ((1, 1), (3, -1), (2, 2)):
        sum_b = sum_b + send(blocks[r], "y", step).astype(F32)

    sums = unturn(sum_a.astype(BF16), sum_b.astype(BF16))
    returned = lax.all_to_all(
        sums.reshape(EXPERTS, CAP, 2 * FEAT), ("x", "c"), split_axis=0, concat_axis=0, tiled=True
    )
    grad_t, curv_t = combine(table, returned.reshape(SLOTS, 2 * FEAT))
    return grad_t.T, curv_t.T


def solution(mesh):
    fine = Mesh(mesh.devices.reshape(4, 2, NZ, NY), ("x", "c", "z", "y"))
    expert, tensor = ("x", "c"), ("z", "y")
    in_specs = (
        P(expert, tensor),
        P(expert, tensor),
        P(expert, tensor),
        P(expert, None),
        P(expert, None),
        P(expert, None, tensor),
        P(expert, None, tensor),
        P(expert, tensor, None),
    )
    out_specs = (P(expert, tensor), P(expert, tensor))
    return jax.shard_map(
        on_device, mesh=fine, in_specs=in_specs, out_specs=out_specs, check_vma=False
    )
```

```python
import functools

import jax
import jax.numpy as jnp
from jax import lax
from jax.experimental import pallas as pl
from jax.experimental.pallas import tpu as pltpu
from jax.sharding import Mesh, PartitionSpec as P

EXPERTS = 8
TOP = 2
CAP = 48
SLOTS = EXPERTS * CAP
NZ = 8
NY = 4
TOK = 128
FEAT = 192
GA = 112
GB = 80
SA = 112
SB = 80
HID = 256
LANES = 128
F32 = jnp.float32
BF16 = jnp.bfloat16
VMEM = 60 * 1024 * 1024
MEDIUM = pl.CostEstimate(flops=12_000_000_000, bytes_accessed=1024, transcendentals=0)
SMALL = pl.CostEstimate(flops=1024, bytes_accessed=1024, transcendentals=0)


def send(block, axis, step):
    n = NZ if axis == "z" else NY
    return lax.ppermute(block, axis, [(i, (i + step) % n) for i in range(n)])


def pack_kernel(ids_ref, prob_ref, tok_ref, tan_ref, cot_ref, out_ref, table_ref):
    ids = ids_ref[...]
    prob = prob_ref[...].astype(F32)
    expert = lax.broadcasted_iota(jnp.int32, (EXPERTS, TOK), 0)
    hits = [(ids[k : k + 1] == expert).astype(F32) for k in range(TOP)]
    row = lax.broadcasted_iota(jnp.int32, (TOK, TOK), 0)
    col = lax.broadcasted_iota(jnp.int32, (TOK, TOK), 1)
    earlier = (row < col).astype(BF16)
    ranks = jnp.dot((hits[0] + hits[1]).astype(BF16), earlier, preferred_element_type=F32)
    slot = lax.broadcasted_iota(jnp.int32, (SLOTS, TOK), 0)
    table = jnp.zeros((SLOTS, TOK), F32)
    weight = jnp.zeros((SLOTS, TOK), F32)
    for k in range(TOP):
        rank = jnp.sum(ranks * hits[k], axis=0, keepdims=True).astype(jnp.int32)
        here = (slot == ids[k : k + 1] * CAP + rank).astype(F32)
        table = table + here
        weight = weight + here * prob[k : k + 1]
    table = table.astype(BF16)
    table_ref[...] = table
    source = jnp.concatenate([tok_ref[...], tan_ref[...], cot_ref[...]], axis=0)
    dims = (((1,), (1,)), ((), ()))
    placed = lax.dot_general(table, source, dims, preferred_element_type=F32)
    ones = jnp.ones((64, TOK), BF16)
    weights = lax.dot_general(weight.astype(BF16), ones, dims, preferred_element_type=F32)
    out_ref[...] = jnp.concatenate([placed.astype(BF16), weights.astype(BF16)], axis=1)


def pack(ids, prob, tok, tan, cot):
    return pl.pallas_call(
        pack_kernel,
        out_shape=(
            jax.ShapeDtypeStruct((SLOTS, 640), BF16),
            jax.ShapeDtypeStruct((SLOTS, TOK), BF16),
        ),
        name="pack",
    )(ids, prob, tok, tan, cot)


def turn_kernel(in_ref, a_ref, b_ref, prob_ref):
    turned = in_ref[...].astype(F32).T
    for i in range(3):
        part = turned[i * FEAT : (i + 1) * FEAT].astype(BF16)
        a_ref[:, i * SLOTS : (i + 1) * SLOTS] = part[:GA]
        b_ref[:, i * SLOTS : (i + 1) * SLOTS] = part[GA:]
    prob_ref[...] = turned[3 * FEAT : 3 * FEAT + 8]


def turn(routed):
    return pl.pallas_call(
        turn_kernel,
        out_shape=(
            jax.ShapeDtypeStruct((GA, 3 * SLOTS), BF16),
            jax.ShapeDtypeStruct((GB, 3 * SLOTS), BF16),
            jax.ShapeDtypeStruct((8, SLOTS), F32),
        ),
        name="turn",
    )(routed)


G_EARLY, S_EARLY = 5, 4
RING = (0, 1, -1, 2, -2, 3, -3, 4)
G_AT = {place: (i - G_EARLY) % NZ for i, place in enumerate(RING)}
S_AT = {place: (i - S_EARLY) % NZ for i, place in enumerate(RING)}


def z_place(i, place, early):
    i = (i + early) % NZ
    return (place[0] + NZ + (i + 1) // 2 * (2 * (i % 2) - 1)) % NZ


def order_kernel(cut, place_ref, *refs):
    a_ref, b_ref = refs[-2:]
    parts = [refs[0][0], refs[1][0]]
    if len(refs) == 5:
        parts.append(refs[2][0].astype(F32).T.astype(BF16))
    rows = jnp.concatenate(parts, axis=1)
    rest = FEAT - cut
    for shift in range(NY):

        @pl.when(place_ref[1] == shift)
        def _():
            for r in range(NY):
                start = (shift + r) % NY * FEAT
                a_ref[r] = rows[start : start + cut]
                b_ref[0, r * rest : (r + 1) * rest] = rows[start + cut : start + FEAT]


def order(place, cut, early, *weights):
    rows, cols, rest = NY * FEAT, len(weights) * HID, FEAT - cut
    tall = pl.BlockSpec((1, rows, HID), lambda i, p: (0, z_place(i, p, early), 0))
    wide = pl.BlockSpec((1, HID, rows), lambda i, p: (0, 0, z_place(i, p, early)))
    return pl.pallas_call(
        functools.partial(order_kernel, cut),
        grid_spec=pltpu.PrefetchScalarGridSpec(
            num_scalar_prefetch=1,
            grid=(NZ,),
            in_specs=[tall, tall, wide][: len(weights)],
            out_specs=[
                pl.BlockSpec((NY, cut, cols), lambda i, p: (0, i, 0)),
                pl.BlockSpec((1, NY * rest, cols), lambda i, p: (i, 0, 0)),
            ],
        ),
        out_shape=(
            jax.ShapeDtypeStruct((NY, NZ * cut, cols), BF16),
            jax.ShapeDtypeStruct((NZ, NY * rest, cols), BF16),
        ),
        compiler_params=pltpu.CompilerParams(vmem_limit_bytes=VMEM),
        cost_estimate=pl.CostEstimate(
            flops=0, bytes_accessed=4 * 6144 * cols, transcendentals=0
        ),
        name="order",
    )(place, *weights)


def flip_kernel(in_ref, *out_refs):
    turned = in_ref[0].astype(F32).T.astype(BF16)
    start = 0
    for out_ref in out_refs:
        width = out_ref.shape[2]
        out_ref[0] = turned[:, start : start + width]
        start += width


def flip(w, *widths):
    n, rows, cols = w.shape
    return pl.pallas_call(
        flip_kernel,
        grid=(n,),
        in_specs=[pl.BlockSpec((1, rows, cols), lambda i: (i, 0, 0))],
        out_specs=[pl.BlockSpec((1, cols, width), lambda i: (i, 0, 0)) for width in widths],
        out_shape=[jax.ShapeDtypeStruct((n, cols, width), BF16) for width in widths],
        compiler_params=pltpu.CompilerParams(vmem_limit_bytes=VMEM),
        cost_estimate=SMALL,
        name="flip",
    )(w)


def unturn_kernel(a_ref, b_ref, out_ref):
    both = jnp.concatenate([a_ref[...], b_ref[...]], axis=0).astype(F32)
    for j in range(SLOTS // LANES):
        rows = slice(j * LANES, (j + 1) * LANES)
        grad = both[:, 2 * j * LANES : (2 * j + 1) * LANES].T
        curv = both[:, (2 * j + 1) * LANES : (2 * j + 2) * LANES].T
        out_ref[rows] = jnp.concatenate([grad, curv], axis=1).astype(BF16)


def unturn(a, b):
    return pl.pallas_call(
        unturn_kernel,
        out_shape=jax.ShapeDtypeStruct((SLOTS, 2 * FEAT), BF16),
        name="unturn",
    )(a, b)


def combine_kernel(table_ref, in_ref, grad_ref, curv_ref):
    sums = in_ref[...].astype(F32).T.astype(BF16)
    total = jnp.dot(sums, table_ref[...], preferred_element_type=F32).astype(BF16)
    grad_ref[...] = total[:FEAT]
    curv_ref[...] = total[FEAT:]


def combine(table, back):
    return pl.pallas_call(
        combine_kernel,
        out_shape=(
            jax.ShapeDtypeStruct((FEAT, TOK), BF16),
            jax.ShapeDtypeStruct((FEAT, TOK), BF16),
        ),
        name="combine",
    )(table, back)


def products(groups, refs, fore, back):
    at = 0
    for ranges in groups:
        w = refs[at][0]
        tok, tan, cot = [
            jnp.concatenate(
                [refs[at + 1 + 3 * n + i][a:b] for n, (a, b) in enumerate(ranges)], axis=0
            )
            for i in range(3)
        ]
        at += 1 + 3 * len(ranges)
        fore = fore + matmul(w[: 2 * HID], jnp.concatenate([tok, tan], axis=1))
        back = back + matmul(w[2 * HID :], cot)
    return fore, back


def absorb_kernel(counts, first, *refs):
    fore_out, back_out = refs[-2:]
    if first:
        fore, back = jnp.zeros(fore_out.shape, F32), jnp.zeros(back_out.shape, F32)
    else:
        fore, back = refs[0][...], refs[1][...]
        refs = refs[2:]
    fore_out[...], back_out[...] = products(counts, refs[:-2], fore, back)


def finish_kernel(counts, fore_ref, back_ref, prob_ref, far_ref, near_ref, wide_ref, *refs):
    out_ref = refs[-5]
    fore, back = products(counts, refs[:-5], fore_ref[...], back_ref[...])
    back = back * prob_ref[:1]
    pre_gate, pre_up = fore[:HID, :LANES], fore[HID:, :LANES]
    tan_gate, tan_up = fore[:HID, LANES:], fore[HID:, LANES:]
    sig = 1.0 / (1.0 + jnp.exp(-pre_gate))
    silu_value = pre_gate * sig
    first = sig * (1.0 + pre_gate * (1.0 - sig))
    second = sig * (1.0 - sig) * (2.0 + pre_gate * (1.0 - 2.0 * sig))
    out_ref[:HID, :LANES] = (back * pre_up * first).astype(BF16)
    out_ref[HID:, :LANES] = (back * silu_value).astype(BF16)
    curv_gate = back * (tan_up * first + pre_up * second * tan_gate)
    out_ref[:HID, LANES:] = curv_gate.astype(BF16)
    out_ref[HID:, LANES:] = (back * first * tan_gate).astype(BF16)
    terms = out_ref[...]
    for weights, first_ref in ((far_ref, refs[-4]), (near_ref, refs[-3])):
        first_ref[...] = matmul(weights[0], terms).astype(BF16)
    far = matmul(wide_ref[0], terms).astype(BF16)
    cut = far.shape[0] // 2
    refs[-2][...] = far[:cut]
    refs[-1][...] = far[cut:]


FORE = pl.BlockSpec((2 * HID, 2 * LANES), lambda j: (0, j))
BACK = pl.BlockSpec((HID, LANES), lambda j: (0, j))
PROB = pl.BlockSpec((8, LANES), lambda j: (0, j))


def operands(groups):
    n = SLOTS // LANES
    specs, arrays = [], []
    for weights, place, pieces in groups:
        specs.append(pl.BlockSpec((1,) + weights.shape[1:], lambda j, r=place: (r, 0, 0)))
        arrays.append(weights)
        for piece, _, _ in pieces:
            for i in range(3):
                block = (piece.shape[0], LANES)
                specs.append(pl.BlockSpec(block, lambda j, i=i: (0, i * n + j)))
                arrays.append(piece)
    return [[piece[1:] for piece in pieces] for _, _, pieces in groups], specs, arrays


def absorb(sums, groups):
    counts, specs, arrays = operands(groups)
    return pl.pallas_call(
        functools.partial(absorb_kernel, counts, sums is None),
        grid=(SLOTS // LANES,),
        in_specs=([] if sums is None else [FORE, BACK]) + specs,
        out_specs=[FORE, BACK],
        out_shape=[
            jax.ShapeDtypeStruct((2 * HID, 2 * SLOTS), F32),
            jax.ShapeDtypeStruct((HID, SLOTS), F32),
        ],
        compiler_params=pltpu.CompilerParams(vmem_limit_bytes=VMEM),
        cost_estimate=SMALL,
        name="absorb",
    )(*(sums or ()), *arrays)


def finish(sums, prob, firsts, groups):
    counts, specs, arrays = operands(groups)
    rows = [n for _, _, n in firsts[:-1]] + [firsts[-1][2] // 2] * 2
    return pl.pallas_call(
        functools.partial(finish_kernel, counts),
        grid=(SLOTS // LANES,),
        in_specs=[
            FORE,
            BACK,
            PROB,
        ]
        + [
            pl.BlockSpec((1, n, 2 * HID), lambda j, place=place: (place, 0, 0))
            for _, place, n in firsts
        ]
        + specs,
        out_specs=[FORE] + [pl.BlockSpec((n, 2 * LANES), lambda j: (0, j)) for n in rows],
        out_shape=[
            jax.ShapeDtypeStruct((n, 2 * SLOTS), BF16) for n in (2 * HID, *rows)
        ],
        compiler_params=pltpu.CompilerParams(vmem_limit_bytes=VMEM),
        cost_estimate=SMALL,
        name="finish",
    )(*sums, prob, *(weights for weights, _, _ in firsts), *arrays)


def after(x, *others):
    return lax.optimization_barrier((x, *others))[0]


def halves(rows):
    return rows // 32 * 16


def total_kernel(own_ref, *refs):
    acc = own_ref[...]
    for ref in refs[:-1]:
        acc = acc + ref[...].astype(F32)
    refs[-1][...] = acc.astype(BF16)


def total(own, moved):
    return pl.pallas_call(
        total_kernel,
        out_shape=jax.ShapeDtypeStruct(own.shape, BF16),
        cost_estimate=MEDIUM,
        name="total",
    )(own, *moved)


def y_both(block):
    return y_both_of(block, block)


def y_both_of(up, down):
    return send(up, "y", 1), send(down, "y", -1)


def matmul(a, b):
    return jnp.dot(a, b, preferred_element_type=F32)


def on_device(tokens, tangent, cotangent, expert_ids, gate_probs, w_gate, w_up, w_down):
    place = jnp.stack([lax.axis_index("z"), lax.axis_index("y")]).astype(jnp.int32)
    packed, table = pack(expert_ids.T, gate_probs.T, tokens.T, tangent.T, cotangent.T)
    routed = lax.all_to_all(
        packed.reshape(EXPERTS, CAP, 640), ("x", "c"), split_axis=0, concat_axis=0, tiled=True
    )
    routed, w1_a, w1_b = lax.optimization_barrier(
        (routed, *order(place, GA, G_EARLY, w_gate, w_up, w_down))
    )
    block_a, block_b, prob = turn(routed.reshape(SLOTS, 640))

    up1, down1 = lax.optimization_barrier((send(block_a, "z", 1), send(block_a, "z", -1)))
    near = [send(after(block_b, up1, down1), "y", step) for step in (1, -1, 2)]
    up2, down2, *near = lax.optimization_barrier((send(up1, "z", 1), send(down1, "z", -1), *near))
    early = jnp.concatenate([block_a, down1, up1, down2, up2], axis=0)
    early_up, early_down = y_both(early)
    up3, down3 = lax.optimization_barrier((send(up2, "z", 1), send(down2, "z", -1)))
    far = send(up3, "z", 1)
    few, many = (NZ - G_EARLY) * GA, G_EARLY * GA
    wide_b = jnp.concatenate([block_b, near[1], near[2], near[0]], axis=0)
    wide_b, w1_a, w1_b, _, _ = lax.optimization_barrier((wide_b, w1_a, w1_b, up3, down3))

    b_up1, b_down1 = send(wide_b, "z", 1), send(wide_b, "z", -1)
    late = [down3, up3, far]
    half = halves(many)
    late_up = jnp.concatenate([early_up[:half], *late], axis=0)
    late_down = jnp.concatenate([early_down[half:], *late], axis=0)
    t_late, t_early = flip(w1_a, few, many)
    (t_b,) = flip(w1_b, NY * GB)
    b_up1, b_down1, t_late, t_early, t_b, late_up, late_down, place = lax.optimization_barrier(
        (b_up1, b_down1, t_late, t_early, t_b, late_up, late_down, place)
    )
    late_up, late_down = send(late_up, "y", 1), send(late_down, "y", -1)

    b_up2, b_down2 = send(b_up1, "z", 1), send(b_down1, "z", -1)
    wide = NY * GB
    sums = absorb(
        None,
        [
            (t_early, 0, [(early, 0, many)]),
            (t_early, 3, [(early_up, 0, many)]),
            (t_early, 1, [(early_down, 0, many)]),
        ],
    )
    w2_a, w2_b = order(place, SA, S_EARLY, w_gate, w_up)
    b_up2, b_down2, w2_a, w2_b, *sums = lax.optimization_barrier(
        (b_up2, b_down2, w2_a, w2_b, *sums)
    )

    b_up3, b_down3 = send(b_up2, "z", 1), send(b_down2, "z", -1)
    sums = absorb(
        sums,
        [
            (t_late, 0, [(block, 0, GA) for block in late]),
            (t_b, G_AT[0], [(wide_b, 0, wide)]),
            (t_b, G_AT[1], [(b_down1, 0, wide)]),
            (t_b, G_AT[-1], [(b_up1, 0, wide)]),
        ],
    )
    sums = absorb(
        sums,
        [(t_b, G_AT[2], [(b_down2, 0, wide)]), (t_b, G_AT[-2], [(b_up2, 0, wide)])],
    )
    rest = many - half
    ends = (half, half + few), (rest, rest + few)
    cut, b_cut = halves(few), halves(wide)
    late_up, late_down, *sums = lax.optimization_barrier((late_up, late_down, *sums))
    late_far_up = send(late_up[half : half + cut], "y", 1)
    late_far_down = send(late_down[rest + cut :], "y", -1)
    b_up3, b_down3, sums = lax.optimization_barrier((b_up3, b_down3, sums))

    b_far_up = send(b_up3[:b_cut], "z", 1)
    b_far_down = send(b_down3[b_cut:], "z", -1)
    sums = absorb(
        sums,
        [
            (t_early, 2, [(late_up, 0, half), (late_down, 0, rest)]),
            (t_late, 3, [(late_up, *ends[0])]),
            (t_late, 1, [(late_down, *ends[1])]),
            (t_b, G_AT[3], [(b_down3, 0, wide)]),
            (t_b, G_AT[-3], [(b_up3, 0, wide)]),
        ],
    )
    last = [
        (t_late, 2, [(late_far_up, 0, cut), (late_far_down, 0, few - cut)]),
        (t_b, G_AT[4], [(b_far_up, 0, b_cut), (b_far_down, 0, wide - b_cut)]),
    ]
    rows, b_cut = NZ * SA // 2, NY * SB // 2
    terms, far_up, late_down, b_up, b_down = finish(
        sums, prob, [(w2_a, 2, rows), (w2_a, 3, rows), (w2_b, S_AT[4], 2 * b_cut)], last
    )

    up, late_down = send(far_up, "y", 1), send(late_down, "y", -1)
    b_up, b_down = lax.optimization_barrier((send(b_up, "z", 1), send(b_down, "z", -1)))
    terms = after(terms, b_up)
    late_up = matmul(w2_a[1, :rows], terms) + up.astype(F32)
    far_down = matmul(w2_a[2, rows:], terms).astype(BF16)
    late_up, far_down, late_down = lax.optimization_barrier(
        (late_up.astype(BF16), far_down, late_down)
    )
    up, down = send(late_up, "y", 1), send(far_down, "y", -1)
    late = matmul(w2_a[0, :rows], terms) + late_down.astype(F32) + up.astype(F32)
    early_up = matmul(w2_a[1, rows:], terms).astype(BF16)
    early_down = (matmul(w2_a[3, rows:], terms) + down.astype(F32)).astype(BF16)
    early_up, early_down, late = lax.optimization_barrier((early_up, early_down, late))
    early_up, early_down = y_both_of(early_up, early_down)

    for step in (3, 2, 1):
        term_up = matmul(w2_b[S_AT[step]], terms)
        term_down = matmul(w2_b[S_AT[-step]], terms)
        b_up, b_down = b_up.astype(F32), b_down.astype(F32)
        if step == 3:
            b_up = jnp.concatenate([term_up[:b_cut] + b_up, term_up[b_cut:]], axis=0)
            b_down = jnp.concatenate([term_down[:b_cut], term_down[b_cut:] + b_down], axis=0)
        else:
            b_up, b_down = term_up + b_up, term_down + b_down
        b_up, b_down = lax.optimization_barrier(
            (send(b_up.astype(BF16), "z", 1), send(b_down.astype(BF16), "z", -1))
        )
    mid_b = matmul(w2_b[S_AT[0]], terms) + b_up.astype(F32) + b_down.astype(F32)

    def late_at(place):
        return late[S_AT[place] * SA : (S_AT[place] + 1) * SA]

    def early_at(place):
        return early[S_AT[place] * SA - rows : (S_AT[place] + 1) * SA - rows]

    up = send(late_at(4).astype(BF16), "z", 1)
    down = send(late_at(-3).astype(BF16), "z", -1)
    up = send((late_at(3) + up.astype(F32)).astype(BF16), "z", 1)
    down = send((late_at(-2) + down.astype(F32)).astype(BF16), "z", -1)
    early = matmul(w2_a[0, rows:], terms) + early_up.astype(F32) + early_down.astype(F32)
    up = send((early_at(2) + up.astype(F32)).astype(BF16), "z", 1)
    down = send((early_at(-1) + down.astype(F32)).astype(BF16), "z", -1)
    up = send((early_at(1) + up.astype(F32)).astype(BF16), "z", 1)
    sum_a = early_at(0) + up.astype(F32) + down.astype(F32)

    blocks = [mid_b[r * SB : (r + 1) * SB] for r in range(NY)]
    moved = [send(blocks[r].astype(BF16), "y", step) for r, step in ((1, 1), (3, -1), (2, 2))]
    sum_b = total(blocks[0], moved)

    sums = unturn(sum_a.astype(BF16), sum_b)
    returned = lax.all_to_all(
        sums.reshape(EXPERTS, CAP, 2 * FEAT), ("x", "c"), split_axis=0, concat_axis=0, tiled=True
    )
    grad_t, curv_t = combine(table, returned.reshape(SLOTS, 2 * FEAT))
    return grad_t.T, curv_t.T


def solution(mesh):
    fine = Mesh(mesh.devices.reshape(4, 2, NZ, NY), ("x", "c", "z", "y"))
    expert, tensor = ("x", "c"), ("z", "y")
    in_specs = (
        P(expert, tensor),
        P(expert, tensor),
        P(expert, tensor),
        P(expert, None),
        P(expert, None),
        P(expert, None, tensor),
        P(expert, None, tensor),
        P(expert, tensor, None),
    )
    out_specs = (P(expert, tensor), P(expert, tensor))
    return jax.shard_map(
        on_device, mesh=fine, in_specs=in_specs, out_specs=out_specs, check_vma=False
    )
```

```python
import functools

import jax
import jax.numpy as jnp
from jax import lax
from jax.experimental import pallas as pl
from jax.experimental.pallas import tpu as pltpu
from jax.sharding import Mesh, PartitionSpec as P

EXPERTS = 8
TOP = 2
CAP = 48
SLOTS = EXPERTS * CAP
NZ = 8
NY = 4
TOK = 128
FEAT = 192
GA = 112
GB = 80
SA = 128
SB = 64
HID = 256
LANES = 128
F32 = jnp.float32
BF16 = jnp.bfloat16
VMEM = 60 * 1024 * 1024
MEDIUM = pl.CostEstimate(flops=12_000_000_000, bytes_accessed=1024, transcendentals=0)
SMALL = pl.CostEstimate(flops=1024, bytes_accessed=1024, transcendentals=0)


def send(block, axis, step):
    n = NZ if axis == "z" else NY
    return lax.ppermute(block, axis, [(i, (i + step) % n) for i in range(n)])


def pack_kernel(ids_ref, prob_ref, tok_ref, tan_ref, cot_ref, out_ref, table_ref):
    ids = ids_ref[...]
    prob = prob_ref[...].astype(F32)
    expert = lax.broadcasted_iota(jnp.int32, (EXPERTS, TOK), 0)
    hits = [(ids[k : k + 1] == expert).astype(F32) for k in range(TOP)]
    row = lax.broadcasted_iota(jnp.int32, (TOK, TOK), 0)
    col = lax.broadcasted_iota(jnp.int32, (TOK, TOK), 1)
    earlier = (row < col).astype(BF16)
    ranks = jnp.dot((hits[0] + hits[1]).astype(BF16), earlier, preferred_element_type=F32)
    slot = lax.broadcasted_iota(jnp.int32, (SLOTS, TOK), 0)
    table = jnp.zeros((SLOTS, TOK), F32)
    weight = jnp.zeros((SLOTS, TOK), F32)
    for k in range(TOP):
        rank = jnp.sum(ranks * hits[k], axis=0, keepdims=True).astype(jnp.int32)
        here = (slot == ids[k : k + 1] * CAP + rank).astype(F32)
        table = table + here
        weight = weight + here * prob[k : k + 1]
    table = table.astype(BF16)
    table_ref[...] = table
    source = jnp.concatenate([tok_ref[...], tan_ref[...], cot_ref[...]], axis=0)
    dims = (((1,), (1,)), ((), ()))
    placed = lax.dot_general(table, source, dims, preferred_element_type=F32)
    ones = jnp.ones((64, TOK), BF16)
    weights = lax.dot_general(weight.astype(BF16), ones, dims, preferred_element_type=F32)
    out_ref[...] = jnp.concatenate([placed.astype(BF16), weights.astype(BF16)], axis=1)


def pack(ids, prob, tok, tan, cot):
    return pl.pallas_call(
        pack_kernel,
        out_shape=(
            jax.ShapeDtypeStruct((SLOTS, 640), BF16),
            jax.ShapeDtypeStruct((SLOTS, TOK), BF16),
        ),
        name="pack",
    )(ids, prob, tok, tan, cot)


def turn_kernel(in_ref, a_ref, b_ref, prob_ref):
    turned = in_ref[...].astype(F32).T
    for i in range(3):
        part = turned[i * FEAT : (i + 1) * FEAT].astype(BF16)
        a_ref[:, i * SLOTS : (i + 1) * SLOTS] = part[:GA]
        b_ref[:, i * SLOTS : (i + 1) * SLOTS] = part[GA:]
    prob_ref[...] = turned[3 * FEAT : 3 * FEAT + 8]


def turn(routed):
    return pl.pallas_call(
        turn_kernel,
        out_shape=(
            jax.ShapeDtypeStruct((GA, 3 * SLOTS), BF16),
            jax.ShapeDtypeStruct((GB, 3 * SLOTS), BF16),
            jax.ShapeDtypeStruct((8, SLOTS), F32),
        ),
        name="turn",
    )(routed)


G_EARLY, S_EARLY = 5, 4
RING = (0, 1, -1, 2, -2, 3, -3, 4)
G_AT = {place: (i - G_EARLY) % NZ for i, place in enumerate(RING)}
S_AT = {place: (i - S_EARLY) % NZ for i, place in enumerate(RING)}


def z_place(i, place, early):
    i = (i + early) % NZ
    return (place[0] + NZ + (i + 1) // 2 * (2 * (i % 2) - 1)) % NZ


def order_kernel(cut, place_ref, *refs):
    a_ref, b_ref = refs[-2:]
    parts = [refs[0][0], refs[1][0]]
    if len(refs) == 5:
        parts.append(refs[2][0].astype(F32).T.astype(BF16))
    rows = jnp.concatenate(parts, axis=1)
    rest = FEAT - cut
    for shift in range(NY):

        @pl.when(place_ref[1] == shift)
        def _():
            for r in range(NY):
                start = (shift + r) % NY * FEAT
                a_ref[r] = rows[start : start + cut]
                b_ref[0, r * rest : (r + 1) * rest] = rows[start + cut : start + FEAT]


def order(place, cut, early, *weights):
    rows, cols, rest = NY * FEAT, len(weights) * HID, FEAT - cut
    tall = pl.BlockSpec((1, rows, HID), lambda i, p: (0, z_place(i, p, early), 0))
    wide = pl.BlockSpec((1, HID, rows), lambda i, p: (0, 0, z_place(i, p, early)))
    return pl.pallas_call(
        functools.partial(order_kernel, cut),
        grid_spec=pltpu.PrefetchScalarGridSpec(
            num_scalar_prefetch=1,
            grid=(NZ,),
            in_specs=[tall, tall, wide][: len(weights)],
            out_specs=[
                pl.BlockSpec((NY, cut, cols), lambda i, p: (0, i, 0)),
                pl.BlockSpec((1, NY * rest, cols), lambda i, p: (i, 0, 0)),
            ],
        ),
        out_shape=(
            jax.ShapeDtypeStruct((NY, NZ * cut, cols), BF16),
            jax.ShapeDtypeStruct((NZ, NY * rest, cols), BF16),
        ),
        compiler_params=pltpu.CompilerParams(vmem_limit_bytes=VMEM),
        cost_estimate=pl.CostEstimate(
            flops=0, bytes_accessed=4 * 6144 * cols, transcendentals=0
        ),
        name="order",
    )(place, *weights)


def flip_kernel(in_ref, *out_refs):
    turned = in_ref[0].astype(F32).T.astype(BF16)
    start = 0
    for out_ref in out_refs:
        width = out_ref.shape[2]
        out_ref[0] = turned[:, start : start + width]
        start += width


def flip(w, *widths, cost=None):
    n, rows, cols = w.shape
    return pl.pallas_call(
        flip_kernel,
        grid=(n,),
        in_specs=[pl.BlockSpec((1, rows, cols), lambda i: (i, 0, 0))],
        out_specs=[pl.BlockSpec((1, cols, width), lambda i: (i, 0, 0)) for width in widths],
        out_shape=[jax.ShapeDtypeStruct((n, cols, width), BF16) for width in widths],
        compiler_params=pltpu.CompilerParams(vmem_limit_bytes=VMEM),
        cost_estimate=cost or SMALL,
        name="flip",
    )(w)


def unturn_kernel(a_ref, b_ref, out_ref):
    both = jnp.concatenate([a_ref[...], b_ref[...]], axis=0).astype(F32)
    for j in range(SLOTS // LANES):
        rows = slice(j * LANES, (j + 1) * LANES)
        grad = both[:, 2 * j * LANES : (2 * j + 1) * LANES].T
        curv = both[:, (2 * j + 1) * LANES : (2 * j + 2) * LANES].T
        out_ref[rows] = jnp.concatenate([grad, curv], axis=1).astype(BF16)


def unturn(a, b):
    return pl.pallas_call(
        unturn_kernel,
        out_shape=jax.ShapeDtypeStruct((SLOTS, 2 * FEAT), BF16),
        name="unturn",
    )(a, b)


def combine_kernel(table_ref, in_ref, grad_ref, curv_ref):
    sums = in_ref[...].astype(F32).T.astype(BF16)
    total = jnp.dot(sums, table_ref[...], preferred_element_type=F32).astype(BF16)
    grad_ref[...] = total[:FEAT]
    curv_ref[...] = total[FEAT:]


def combine(table, back):
    return pl.pallas_call(
        combine_kernel,
        out_shape=(
            jax.ShapeDtypeStruct((FEAT, TOK), BF16),
            jax.ShapeDtypeStruct((FEAT, TOK), BF16),
        ),
        name="combine",
    )(table, back)


def products(groups, refs, fore, back):
    at = 0
    for ranges in groups:
        w = refs[at][0]
        tok, tan, cot = [
            jnp.concatenate(
                [refs[at + 1 + 3 * n + i][a:b] for n, (a, b) in enumerate(ranges)], axis=0
            )
            for i in range(3)
        ]
        at += 1 + 3 * len(ranges)
        fore = fore + matmul(w[: 2 * HID], jnp.concatenate([tok, tan], axis=1))
        back = back + matmul(w[2 * HID :], cot)
    return fore, back


def absorb_kernel(counts, first, *refs):
    fore_out, back_out = refs[-2:]
    if first:
        fore, back = jnp.zeros(fore_out.shape, F32), jnp.zeros(back_out.shape, F32)
    else:
        fore, back = refs[0][...], refs[1][...]
        refs = refs[2:]
    fore_out[...], back_out[...] = products(counts, refs[:-2], fore, back)


def finish_kernel(counts, fore_ref, back_ref, prob_ref, far_ref, near_ref, wide_ref, *refs):
    out_ref = refs[-5]
    fore, back = products(counts, refs[:-5], fore_ref[...], back_ref[...])
    back = back * prob_ref[:1]
    pre_gate, pre_up = fore[:HID, :LANES], fore[HID:, :LANES]
    tan_gate, tan_up = fore[:HID, LANES:], fore[HID:, LANES:]
    sig = 1.0 / (1.0 + jnp.exp(-pre_gate))
    silu_value = pre_gate * sig
    first = sig * (1.0 + pre_gate * (1.0 - sig))
    second = sig * (1.0 - sig) * (2.0 + pre_gate * (1.0 - 2.0 * sig))
    out_ref[:HID, :LANES] = (back * pre_up * first).astype(BF16)
    out_ref[HID:, :LANES] = (back * silu_value).astype(BF16)
    curv_gate = back * (tan_up * first + pre_up * second * tan_gate)
    out_ref[:HID, LANES:] = curv_gate.astype(BF16)
    out_ref[HID:, LANES:] = (back * first * tan_gate).astype(BF16)
    terms = out_ref[...]
    for weights, first_ref in ((far_ref, refs[-4]), (near_ref, refs[-3])):
        first_ref[...] = matmul(weights[0], terms).astype(BF16)
    far = matmul(wide_ref[0], terms).astype(BF16)
    cut = far.shape[0] // 2
    refs[-2][...] = far[:cut]
    refs[-1][...] = far[cut:]


FORE = pl.BlockSpec((2 * HID, 2 * LANES), lambda j: (0, j))
BACK = pl.BlockSpec((HID, LANES), lambda j: (0, j))
PROB = pl.BlockSpec((8, LANES), lambda j: (0, j))


def operands(groups):
    n = SLOTS // LANES
    specs, arrays = [], []
    for weights, place, pieces in groups:
        specs.append(pl.BlockSpec((1,) + weights.shape[1:], lambda j, r=place: (r, 0, 0)))
        arrays.append(weights)
        for piece, _, _ in pieces:
            for i in range(3):
                block = (piece.shape[0], LANES)
                specs.append(pl.BlockSpec(block, lambda j, i=i: (0, i * n + j)))
                arrays.append(piece)
    return [[piece[1:] for piece in pieces] for _, _, pieces in groups], specs, arrays


def absorb(sums, groups):
    counts, specs, arrays = operands(groups)
    return pl.pallas_call(
        functools.partial(absorb_kernel, counts, sums is None),
        grid=(SLOTS // LANES,),
        in_specs=([] if sums is None else [FORE, BACK]) + specs,
        out_specs=[FORE, BACK],
        out_shape=[
            jax.ShapeDtypeStruct((2 * HID, 2 * SLOTS), F32),
            jax.ShapeDtypeStruct((HID, SLOTS), F32),
        ],
        compiler_params=pltpu.CompilerParams(vmem_limit_bytes=VMEM),
        cost_estimate=SMALL,
        name="absorb",
    )(*(sums or ()), *arrays)


def finish(sums, prob, firsts, groups):
    counts, specs, arrays = operands(groups)
    rows = [n for _, _, n in firsts[:-1]] + [firsts[-1][2] // 2] * 2
    return pl.pallas_call(
        functools.partial(finish_kernel, counts),
        grid=(SLOTS // LANES,),
        in_specs=[
            FORE,
            BACK,
            PROB,
        ]
        + [
            pl.BlockSpec((1, n, 2 * HID), lambda j, place=place: (place, 0, 0))
            for _, place, n in firsts
        ]
        + specs,
        out_specs=[FORE] + [pl.BlockSpec((n, 2 * LANES), lambda j: (0, j)) for n in rows],
        out_shape=[
            jax.ShapeDtypeStruct((n, 2 * SLOTS), BF16) for n in (2 * HID, *rows)
        ],
        compiler_params=pltpu.CompilerParams(vmem_limit_bytes=VMEM),
        cost_estimate=SMALL,
        name="finish",
    )(*sums, prob, *(weights for weights, _, _ in firsts), *arrays)


def after(x, *others):
    return lax.optimization_barrier((x, *others))[0]


def halves(rows):
    return rows // 32 * 16


def total_kernel(own_ref, *refs):
    acc = own_ref[...]
    for ref in refs[:-1]:
        acc = acc + ref[...].astype(F32)
    refs[-1][...] = acc.astype(BF16)


def total(own, moved):
    return pl.pallas_call(
        total_kernel,
        out_shape=jax.ShapeDtypeStruct(own.shape, BF16),
        cost_estimate=MEDIUM,
        name="total",
    )(own, *moved)


def y_both(block):
    return y_both_of(block, block)


def y_both_of(up, down):
    return send(up, "y", 1), send(down, "y", -1)


def matmul(a, b):
    return jnp.dot(a, b, preferred_element_type=F32)


def on_device(tokens, tangent, cotangent, expert_ids, gate_probs, w_gate, w_up, w_down):
    place = jnp.stack([lax.axis_index("z"), lax.axis_index("y")]).astype(jnp.int32)
    packed, table = pack(expert_ids.T, gate_probs.T, tokens.T, tangent.T, cotangent.T)
    routed = lax.all_to_all(
        packed.reshape(EXPERTS, CAP, 640), ("x", "c"), split_axis=0, concat_axis=0, tiled=True
    )
    routed, w1_a, w1_b = lax.optimization_barrier(
        (routed, *order(place, GA, G_EARLY, w_gate, w_up, w_down))
    )
    block_a, block_b, prob = turn(routed.reshape(SLOTS, 640))

    few, many = (NZ - G_EARLY) * GA, G_EARLY * GA
    t_late, t_early = flip(after(w1_a, block_a), few, many, cost=MEDIUM)
    up1, down1, t_late, t_early = lax.optimization_barrier(
        (send(block_a, "z", 1), send(block_a, "z", -1), t_late, t_early)
    )
    near = [send(after(block_b, up1, down1), "y", step) for step in (1, -1, 2)]
    up2, down2, *near = lax.optimization_barrier((send(up1, "z", 1), send(down1, "z", -1), *near))
    early = jnp.concatenate([block_a, down1, up1, down2, up2], axis=0)
    early_up, early_down = lax.optimization_barrier(y_both(early))
    up3, down3 = lax.optimization_barrier((send(up2, "z", 1), send(down2, "z", -1)))
    far = send(up3, "z", 1)
    wide_b = jnp.concatenate([block_b, near[1], near[2], near[0]], axis=0)
    wide_b, w1_b, place, _, _ = lax.optimization_barrier((wide_b, w1_b, place, up3, down3))

    b_up1, b_down1 = send(wide_b, "z", 1), send(wide_b, "z", -1)
    late = [down3, up3, far]
    half = halves(many)
    late_up = jnp.concatenate([early_up[:half], *late], axis=0)
    late_down = jnp.concatenate([early_down[half:], *late], axis=0)
    (t_b,) = flip(w1_b, NY * GB)
    w2_a, w2_b = order(place, SA, S_EARLY, w_gate, w_up)
    b_up1, b_down1, t_b, w2_a, w2_b = lax.optimization_barrier((b_up1, b_down1, t_b, w2_a, w2_b))
    t_early = after(t_early, b_up1, late_up, late_down)
    late_up, late_down = send(late_up, "y", 1), send(late_down, "y", -1)

    b_up2, b_down2 = send(b_up1, "z", 1), send(b_down1, "z", -1)
    wide = NY * GB
    sums = absorb(
        None,
        [
            (t_early, 0, [(early, 0, many)]),
            (t_early, 3, [(early_up, 0, many)]),
            (t_early, 1, [(early_down, 0, many)]),
        ],
    )
    b_up2, b_down2, *sums = lax.optimization_barrier((b_up2, b_down2, *sums))

    b_up3, b_down3 = send(b_up2, "z", 1), send(b_down2, "z", -1)
    sums = absorb(
        sums,
        [
            (t_late, 0, [(block, 0, GA) for block in late]),
            (t_b, G_AT[0], [(wide_b, 0, wide)]),
            (t_b, G_AT[1], [(b_down1, 0, wide)]),
            (t_b, G_AT[-1], [(b_up1, 0, wide)]),
        ],
    )
    sums = absorb(
        sums,
        [(t_b, G_AT[2], [(b_down2, 0, wide)]), (t_b, G_AT[-2], [(b_up2, 0, wide)])],
    )
    rest = many - half
    ends = (half, half + few), (rest, rest + few)
    cut, b_cut = halves(few), halves(wide)
    late_up, late_down, *sums = lax.optimization_barrier((late_up, late_down, *sums))
    late_far_up = send(late_up[half : half + cut], "y", 1)
    late_far_down = send(late_down[rest + cut :], "y", -1)
    b_up3, b_down3, sums = lax.optimization_barrier((b_up3, b_down3, sums))

    b_far_up = send(b_up3[:b_cut], "z", 1)
    b_far_down = send(b_down3[b_cut:], "z", -1)
    sums = absorb(
        sums,
        [
            (t_early, 2, [(late_up, 0, half), (late_down, 0, rest)]),
            (t_late, 3, [(late_up, *ends[0])]),
            (t_late, 1, [(late_down, *ends[1])]),
            (t_b, G_AT[3], [(b_down3, 0, wide)]),
            (t_b, G_AT[-3], [(b_up3, 0, wide)]),
        ],
    )
    last = [
        (t_late, 2, [(late_far_up, 0, cut), (late_far_down, 0, few - cut)]),
        (t_b, G_AT[4], [(b_far_up, 0, b_cut), (b_far_down, 0, wide - b_cut)]),
    ]
    rows, b_cut = NZ * SA // 2, NY * SB // 2
    terms, far_up, late_down, b_up, b_down = finish(
        sums, prob, [(w2_a, 2, rows), (w2_a, 3, rows), (w2_b, S_AT[4], 2 * b_cut)], last
    )

    up, late_down = send(far_up, "y", 1), send(late_down, "y", -1)
    b_up, b_down = lax.optimization_barrier((send(b_up, "z", 1), send(b_down, "z", -1)))
    terms = after(terms, b_up)
    late_up = matmul(w2_a[1, :rows], terms) + up.astype(F32)
    far_down = matmul(w2_a[2, rows:], terms).astype(BF16)
    late_up, far_down, late_down = lax.optimization_barrier(
        (late_up.astype(BF16), far_down, late_down)
    )
    up, down = send(late_up, "y", 1), send(far_down, "y", -1)
    late = matmul(w2_a[0, :rows], terms) + late_down.astype(F32) + up.astype(F32)
    early_up = matmul(w2_a[1, rows:], terms).astype(BF16)
    early_down = (matmul(w2_a[3, rows:], terms) + down.astype(F32)).astype(BF16)
    early_up, early_down, late = lax.optimization_barrier((early_up, early_down, late))
    early_up, early_down = y_both_of(early_up, early_down)

    for step in (3, 2, 1):
        term_up = matmul(w2_b[S_AT[step]], terms)
        term_down = matmul(w2_b[S_AT[-step]], terms)
        b_up, b_down = b_up.astype(F32), b_down.astype(F32)
        if step == 3:
            b_up = jnp.concatenate([term_up[:b_cut] + b_up, term_up[b_cut:]], axis=0)
            b_down = jnp.concatenate([term_down[:b_cut], term_down[b_cut:] + b_down], axis=0)
        else:
            b_up, b_down = term_up + b_up, term_down + b_down
        b_up, b_down = lax.optimization_barrier(
            (send(b_up.astype(BF16), "z", 1), send(b_down.astype(BF16), "z", -1))
        )
    mid_b = matmul(w2_b[S_AT[0]], terms) + b_up.astype(F32) + b_down.astype(F32)

    def late_at(place):
        return late[S_AT[place] * SA : (S_AT[place] + 1) * SA]

    def early_at(place):
        return early[S_AT[place] * SA - rows : (S_AT[place] + 1) * SA - rows]

    up = send(late_at(4).astype(BF16), "z", 1)
    down = send(late_at(-3).astype(BF16), "z", -1)
    up = send((late_at(3) + up.astype(F32)).astype(BF16), "z", 1)
    down = send((late_at(-2) + down.astype(F32)).astype(BF16), "z", -1)
    early = matmul(w2_a[0, rows:], terms) + early_up.astype(F32) + early_down.astype(F32)
    up = send((early_at(2) + up.astype(F32)).astype(BF16), "z", 1)
    down = send((early_at(-1) + down.astype(F32)).astype(BF16), "z", -1)
    up = send((early_at(1) + up.astype(F32)).astype(BF16), "z", 1)
    sum_a = early_at(0) + up.astype(F32) + down.astype(F32)

    blocks = [mid_b[r * SB : (r + 1) * SB] for r in range(NY)]
    moved = [send(blocks[r].astype(BF16), "y", step) for r, step in ((1, 1), (3, -1), (2, 2))]
    sum_b = total(blocks[0], moved)

    sums = unturn(sum_a.astype(BF16), sum_b)
    returned = lax.all_to_all(
        sums.reshape(EXPERTS, CAP, 2 * FEAT), ("x", "c"), split_axis=0, concat_axis=0, tiled=True
    )
    grad_t, curv_t = combine(table, returned.reshape(SLOTS, 2 * FEAT))
    return grad_t.T, curv_t.T


def solution(mesh):
    fine = Mesh(mesh.devices.reshape(4, 2, NZ, NY), ("x", "c", "z", "y"))
    expert, tensor = ("x", "c"), ("z", "y")
    in_specs = (
        P(expert, tensor),
        P(expert, tensor),
        P(expert, tensor),
        P(expert, None),
        P(expert, None),
        P(expert, None, tensor),
        P(expert, None, tensor),
        P(expert, tensor, None),
    )
    out_specs = (P(expert, tensor), P(expert, tensor))
    return jax.shard_map(
        on_device, mesh=fine, in_specs=in_specs, out_specs=out_specs, check_vma=False
    )
```
